32 devices in a mesh: band: 8 (over y, x, core), slab: 4 (over z).
Axes of the slice: x: 2, y: 2, z: 4, core: 2. Of those that a mesh axis runs over, the one named last changes fastest.
Arguments:
- orbitals: float32 [8, 128, 128, 128], P('band', 'slab'), may hold values from -6 to 6
- column_ids: int32 [4, 1536], P('slab'), may hold values from 0 to 4095, as said below
- source_ids: int32 [2], replicated, may hold values from 0 to 7
Outputs:
- exchange: float32 [8, 128, 128, 128], P('band', 'slab')
- energy: float32 [8, 6144], P('band', 'slab')
The draws below stay inside these ranges and needn't reach their ends.
Inputs may be any that keep to these rules, and one draw needn't show every extreme that they name: `column_ids`: A column is numbered c = (ky + 32) * 64 + kz + 32. Every column with ky^2 + kz^2 < 32^2 appears exactly once in the whole table; every other slot holds 0, a column outside that disk. One row holds 1536 such disk columns.
All inputs are finite; a program needn't handle non-finite values.
Results may differ from the reference program's by a relative error of at most 0.0001.
Values sent between devices are 32-bit elements; how exact they have to be, the bound alone decides.
A program may use at most 128 MiB of HBM per device.

```python
import jax
import jax.numpy as jnp
import numpy as np
from jax import lax

G = 128
KCUT = 32
KB = 64
CMAX = 1536
ORBITALS = 8
SOURCES = 2
N_SLAB = 4


def draw_column_ids(key, part):
    wave = np.arange(KB) - KCUT
    inside = (wave[:, None] ** 2 + wave[None, :] ** 2 < KCUT * KCUT).reshape(-1)
    disk_count = int(np.sum(inside))
    outside_score = jnp.asarray(1 - inside.astype(np.int32), dtype=jnp.int32)
    disk_ids = jnp.argsort(outside_score, stable=True)[:disk_count].astype(jnp.int32)
    key_order, key_heavy = jax.random.split(jax.random.fold_in(key, 11))
    shuffled = jax.random.permutation(key_order, disk_ids)
    heavy = jax.random.randint(key_heavy, (), 0, N_SLAB, dtype=jnp.int32)
    ranks = jnp.arange(disk_count, dtype=jnp.int32)
    others = (heavy + 1 + (ranks - CMAX) % (N_SLAB - 1)) % N_SLAB
    owner = jnp.where(ranks < CMAX, heavy, others)
    slot = jnp.where(ranks < CMAX, ranks, (ranks - CMAX) // (N_SLAB - 1))
    table = jnp.zeros((N_SLAB, CMAX), jnp.int32)
    return table.at[owner, slot].set(shuffled)


def shard_levels(key, shape, cuts, least, high):
    def one(dim, blocks):
        steps = jax.random.uniform(jax.random.fold_in(jax.random.fold_in(key, 6), dim), (blocks,), jnp.float32, least / len(cuts), high / len(cuts))
        return jnp.repeat(jnp.exp(steps), shape[dim] // blocks).reshape((-1,) + (1,) * (len(shape) - dim - 1))

    loudness = one(*cuts[0])
    for cut in cuts[1:]:
        loudness = loudness * one(*cut)
    return loudness


def bell_draw(key, dims, spread, reach, shards=(), kind=jnp.bfloat16):
    values = jax.random.normal(key, dims, jnp.float32) * spread
    if len(shards) > 0:
        values = shard_levels(key, dims, shards, -0.22, 0.18) * values
    return jnp.clip(values, min=-reach, max=reach).astype(kind)


def setup_inputs(seed: int = 0) -> dict:
    seeds = jax.random.split(jax.random.key(seed), 4)
    return {
        "orbitals": bell_draw(seeds[0], (ORBITALS, G, G, G), 1.0, 6.0, ((0, 8), (1, 4)), jnp.float32),
        "column_ids": draw_column_ids(jax.random.fold_in(seeds[3], 71), 0),
        "source_ids": jax.random.randint(seeds[2], (SOURCES,), 0, ORBITALS).astype(jnp.int32),
    }


def reference(orbitals, column_ids, source_ids):
    wave = (jnp.arange(G, dtype=jnp.int32) + G // 2) % G - G // 2
    half_wave = jnp.arange(G // 2 + 1, dtype=jnp.int32)
    radius = wave[:, None, None] ** 2 + wave[None, :, None] ** 2 + half_wave[None, None, :] ** 2
    kernel_table = jnp.where(radius < KCUT * KCUT, 4.0 / (1.0 + radius.astype(jnp.float32) / 1024.0), 0.0).astype(jnp.float32)
    scale = float(G) ** 1.5
    sources = orbitals[source_ids]

    def per_orbital(orbital):
        def per_source(carry, source):
            exchange, col_power = carry
            spectrum = jnp.fft.rfftn(source * orbital) / scale
            potential = jnp.fft.irfftn(spectrum * kernel_table, s=(G, G, G)) * scale
            magnitude = spectrum.real * spectrum.real + spectrum.imag * spectrum.imag
            col_power = col_power + jnp.sum(kernel_table * magnitude, axis=0) / KB
            return (exchange + source * potential, col_power), None

        start = (jnp.zeros((G, G, G), jnp.float32), jnp.zeros((G, G // 2 + 1), jnp.float32))
        result, _ = lax.scan(per_source, start, sources)
        return result

    exchange, col_power = lax.map(per_orbital, orbitals)
    slot_ids = column_ids.reshape(-1).astype(jnp.int32)
    wave_y = slot_ids // KB - KCUT
    wave_z = slot_ids % KB - KCUT
    flipped = wave_z < 0
    row_index = jnp.where(flipped, (-wave_y) % G, wave_y % G).astype(jnp.int32)
    col_index = jnp.where(flipped, -wave_z, wave_z).astype(jnp.int32)
    energy = col_power[:, row_index, col_index]
    return exchange, energy
```

```python
import functools

import jax
import jax.numpy as jnp
import ml_dtypes
import numpy as np
from jax import lax
from jax.experimental import pallas as pl
from jax.experimental.pallas import tpu as pltpu
from jax.sharding import PartitionSpec as P

KCUT = 32
KB = 64
KH = 32
ROWS = 8
F32 = jnp.float32
BF16 = jnp.bfloat16


def halves(table):
    table = table.astype(np.float32)
    high = table.astype(ml_dtypes.bfloat16)
    low = (table - high.astype(np.float32)).astype(ml_dtypes.bfloat16)
    return high, low


def tables(points):
    wave = np.arange(KB) - KCUT
    angle = (wave[:, None] * np.arange(points)[None, :] % points) * (2.0 * np.pi / points)
    forward = np.concatenate([np.cos(angle), np.sin(angle)], axis=0)
    backward = np.concatenate([np.cos(angle).T, np.sin(angle).T], axis=1)
    angle = (np.arange(KH)[:, None] * np.arange(points)[None, :] % points) * (2.0 * np.pi / points)
    unitary = float(points) ** (-1.5)
    cos_z, sin_z = np.cos(angle) * unitary, np.sin(angle) * unitary
    none = np.zeros_like(cos_z)
    into = np.concatenate(
        [
            np.concatenate([cos_z, none, -sin_z, none], axis=0).T,
            np.concatenate([none, cos_z, none, -sin_z], axis=0).T,
        ],
        axis=0,
    )
    twice = np.where(np.arange(KH) == 0, 1.0, 2.0)[:, None]
    cos_b, sin_b = cos_z * twice, sin_z * twice
    out = np.concatenate(
        [
            np.concatenate([cos_b, none, -sin_b, none], axis=0),
            np.concatenate([none, cos_b, none, -sin_b], axis=0),
        ],
        axis=1,
    )
    fh, fl = halves(forward)
    bh, bl = halves(backward)
    ih, il = halves(into)
    oh, ol = halves(out)
    return (np.concatenate([fh, fl], 0), np.concatenate([bh, bl], 0), ih, il, oh, ol)


def split(value):
    high = value.astype(BF16)
    return high, (value - high.astype(F32)).astype(BF16)


def mm(a, b):
    return jnp.dot(a, b, preferred_element_type=F32)


def left_apply(table_ref, value):
    rows = table_ref.shape[0] // 2
    high, low = split(value)
    both = mm(table_ref[...], high)
    return both[:rows] + both[rows:] + mm(table_ref[:rows, :], low)


def swap_parts(value, sign):
    half = value.shape[1] // 2
    lane = lax.broadcasted_iota(jnp.int32, value.shape, 1)
    rolled = pltpu.roll(value, half, 1)
    return jnp.where(lane < half, sign * rolled, -sign * rolled)


def to_waves(table_ref, value):
    both = left_apply(table_ref, value)
    return both[:KB] + swap_parts(both[KB:], 1.0)


def to_points(table_ref, value):
    return left_apply(table_ref, jnp.concatenate([value, swap_parts(value, -1.0)], axis=0))


def kernel(
    slabs, orb, src, ids, fw, bw, zih, zil, zoh, zol, exch, energy,
    send1, recv1, send2, recv2, powers, s1, r1, s2, r2, sp, rp, own,
):
    planes, points = orb.shape[0], orb.shape[1]
    chunks = planes // ROWS
    width = KB // slabs
    me = lax.axis_index("slab")

    def peer(step):
        return {"slab": lax.rem(me + step, slabs)}

    barrier = pltpu.get_barrier_semaphore()
    for step in range(1, slabs):
        pl.semaphore_signal(barrier, inc=1, device_id=peer(step), device_id_type=pl.DeviceIdType.MESH)
    pl.semaphore_wait(barrier, slabs - 1)

    forward = []
    for chunk in range(chunks):

        def group(part, carry, chunk=chunk):
            base = chunk * ROWS + part * 4
            here = orb[pl.ds(base, 4)].reshape(4 * points, points)
            h0, l0 = split(src[0, pl.ds(base, 4)].reshape(4 * points, points) * here)
            h1, l1 = split(src[1, pl.ds(base, 4)].reshape(4 * points, points) * here)
            high = jnp.concatenate([h0, h1], axis=1)
            low = jnp.concatenate([l0, l1], axis=1)
            along_z = mm(high, zih[...]) + mm(low, zih[...]) + mm(high, zil[...])
            for q in range(4):
                waves = to_waves(fw, along_z[q * points : (q + 1) * points])
                send1[pl.ds(chunk * KB * ROWS + part * 4 + q, KB, stride=ROWS), :] = waves
            return carry

        lax.fori_loop(0, ROWS // 4, group, 0)
        for step in list(range(1, slabs)) + [0]:
            to = lax.rem(me + step, slabs)
            first = pl.multiple_of(chunk * KB * ROWS + to * (width * ROWS), 8)
            source = send1.at[pl.ds(first, width * ROWS)]
            target = recv1.at[me * chunks + chunk]
            if step == 0:
                copy = pltpu.make_async_copy(source, target, own.at[0, chunk])
            else:
                copy = pltpu.make_async_remote_copy(
                    source, target, s1.at[chunk, step], r1.at[chunk, step],
                    device_id=peer(step), device_id_type=pl.DeviceIdType.MESH,
                )
            copy.start()
            forward.append(copy)
    for copy in forward:
        copy.wait()

    lane_z = lax.broadcasted_iota(jnp.int32, (KB, 2 * KB), 1) & (KH - 1)
    wave_x = lax.broadcasted_iota(jnp.int32, (KB, 2 * KB), 0) - KCUT
    flat = wave_x * wave_x + lane_z * lane_z

    def column(k, carry):
        rows = pl.ds(pl.multiple_of(k * ROWS, ROWS), ROWS)
        spectrum = to_waves(fw, recv1[:, rows, :].reshape(points, 2 * KB))
        wave_y = me * width + k - KCUT
        radius = flat + wave_y * wave_y
        weight = jnp.where(radius < KCUT * KCUT, 4.0 / (1.0 + radius.astype(F32) / 1024.0), 0.0)
        filtered = weight * spectrum
        powers[me, pl.ds(k, 1), :] = jnp.sum(filtered * spectrum, axis=0, keepdims=True)
        send2[:, rows, :] = to_points(bw, filtered).reshape(slabs * chunks, ROWS, 2 * KB)
        return carry

    lax.fori_loop(0, width, column, 0, unroll=4)

    back = []
    for chunk in range(chunks):
        waits = []
        for step in list(range(1, slabs)) + [0]:
            to = lax.rem(me + step, slabs)
            first = pl.multiple_of(chunk * KB * ROWS + me * (width * ROWS), 8)
            source = send2.at[to * chunks + chunk]
            target = recv2.at[pl.ds(first, width * ROWS)]
            if step == 0:
                copy = pltpu.make_async_copy(source, target, own.at[1, chunk])
            else:
                copy = pltpu.make_async_remote_copy(
                    source, target, s2.at[chunk, step], r2.at[chunk, step],
                    device_id=peer(step), device_id_type=pl.DeviceIdType.MESH,
                )
            copy.start()
            waits.append(copy)
        back.append(waits)
        if chunk == 0:
            shared = []
            for step in range(1, slabs):
                copy = pltpu.make_async_remote_copy(
                    powers.at[me], powers.at[me], sp.at[step], rp.at[step],
                    device_id=peer(step), device_id_type=pl.DeviceIdType.MESH,
                )
                copy.start()
                shared.append(copy)
    for copy in shared:
        copy.wait()

    power = powers[...].reshape(KB, 2 * KB) * (1.0 / KB)
    slots = ids[...]
    wave_y = (slots >> 6) - KCUT
    wave_z = (slots & (KB - 1)) - KCUT
    wave_y = jnp.where(wave_z < 0, -wave_y, wave_y)
    wave_z = jnp.where(wave_z < 0, -wave_z, wave_z)
    count = slots.shape[1]
    row = lax.broadcasted_iota(jnp.int32, (KB, count), 0) - KCUT
    pick_y = jnp.where(row == wave_y, 1.0, 0.0).astype(BF16)
    row = lax.broadcasted_iota(jnp.int32, (2 * KB, count), 0) & (KH - 1)
    high, low = split(power.T)
    rows_of = mm(high, pick_y) + mm(low, pick_y)
    energy[...] = jnp.sum(jnp.where(row == wave_z, rows_of, 0.0), axis=0, keepdims=True)

    for chunk in range(chunks):
        for copy in back[chunk]:
            copy.wait()

        def ungroup(part, carry, chunk=chunk):
            base = chunk * ROWS + part * 4
            pieces = []
            for q in range(4):
                waves = recv2[pl.ds(chunk * KB * ROWS + part * 4 + q, KB, stride=ROWS), :]
                pieces.append(to_points(bw, waves))
            high, low = split(jnp.concatenate(pieces, axis=0))
            both = mm(high, zoh[...]) + mm(low, zoh[...]) + mm(high, zol[...])
            first = src[0, pl.ds(base, 4)].reshape(4 * points, points)
            second = src[1, pl.ds(base, 4)].reshape(4 * points, points)
            total = first * both[:, :points] + second * both[:, points:]
            exch[pl.ds(base, 4)] = total.reshape(4, points, points)
            return carry

        lax.fori_loop(0, ROWS // 4, ungroup, 0)


def from_root(shard, axis, root):
    mine = lax.axis_index(axis) == root
    return lax.psum(jnp.where(mine, shard, jnp.zeros_like(shard)), axis)


def body(orbitals, column_ids, source_ids):
    slabs = lax.axis_size("slab")
    planes, points = orbitals.shape[1], orbitals.shape[2]
    chunks = planes // ROWS
    width = KB // slabs
    sources = jnp.stack([from_root(orbitals[0], "band", source_ids[i]) for i in range(2)])
    vmem = pl.BlockSpec(memory_space=pltpu.VMEM)
    dma = pltpu.SemaphoreType.DMA
    exchange, energy = pl.pallas_call(
        functools.partial(kernel, slabs),
        out_shape=(
            jax.ShapeDtypeStruct((planes, points, points), F32),
            jax.ShapeDtypeStruct((1, column_ids.shape[1]), F32),
        ),
        in_specs=[vmem] * 9,
        out_specs=(vmem, vmem),
        scratch_shapes=[
            pltpu.VMEM((chunks * KB * ROWS, 2 * KB), F32),
            pltpu.VMEM((slabs * chunks, width * ROWS, 2 * KB), F32),
            pltpu.VMEM((slabs * chunks, width * ROWS, 2 * KB), F32),
            pltpu.VMEM((chunks * KB * ROWS, 2 * KB), F32),
            pltpu.VMEM((slabs, width, 2 * KB), F32),
            dma((chunks, slabs)),
            dma((chunks, slabs)),
            dma((chunks, slabs)),
            dma((chunks, slabs)),
            dma((slabs,)),
            dma((slabs,)),
            dma((2, chunks)),
        ],
        compiler_params=pltpu.CompilerParams(
            collective_id=0, has_side_effects=True, vmem_limit_bytes=48 * 1024 * 1024
        ),
        name="exchange_action",
    )(orbitals[0], sources, column_ids, *[jnp.asarray(t) for t in tables(points)])
    return exchange[None], energy


def solution(mesh):
    placed = (P("band", "slab", None, None), P("slab", None), P())
    return jax.shard_map(
        body,
        mesh=mesh,
        in_specs=placed,
        out_specs=(P("band", "slab", None, None), P("band", "slab")),
        check_vma=False,
    )
```

```python
import functools

import jax
import jax.numpy as jnp
import ml_dtypes
import numpy as np
from jax import lax
from jax.experimental import pallas as pl
from jax.experimental.pallas import tpu as pltpu
from jax.sharding import PartitionSpec as P

KCUT = 32
KB = 64
KH = 32
ROWS = 8
STAGES = 6
F32 = jnp.float32
BF16 = jnp.bfloat16


def halves(table):
    table = table.astype(np.float32)
    high = table.astype(ml_dtypes.bfloat16)
    low = (table - high.astype(np.float32)).astype(ml_dtypes.bfloat16)
    return high, low


def tables(points):
    wave = np.arange(KB) - KCUT
    angle = (wave[:, None] * np.arange(points)[None, :] % points) * (2.0 * np.pi / points)
    forward = np.concatenate([np.cos(angle), np.sin(angle)], axis=0)
    backward = np.concatenate([np.cos(angle).T, np.sin(angle).T], axis=1)
    angle = (np.arange(KH)[:, None] * np.arange(points)[None, :] % points) * (2.0 * np.pi / points)
    unitary = float(points) ** (-1.5)
    cos_z, sin_z = np.cos(angle) * unitary, np.sin(angle) * unitary
    none = np.zeros_like(cos_z)
    into = np.concatenate(
        [
            np.concatenate([cos_z, none, -sin_z, none], axis=0).T,
            np.concatenate([none, cos_z, none, -sin_z], axis=0).T,
        ],
        axis=0,
    )
    twice = np.where(np.arange(KH) == 0, 1.0, 2.0)[:, None]
    cos_b, sin_b = cos_z * twice, sin_z * twice
    out = np.concatenate(
        [
            np.concatenate([cos_b, none, -sin_b, none], axis=0),
            np.concatenate([none, cos_b, none, -sin_b], axis=0),
        ],
        axis=1,
    )
    fh, fl = halves(forward)
    bh, bl = halves(backward)
    ih, il = halves(into)
    oh, ol = halves(out)
    return (np.concatenate([fh, fl], 0), np.concatenate([bh, bl], 0), ih, il, oh, ol)


def split(value):
    high = value.astype(BF16)
    return high, (value - high.astype(F32)).astype(BF16)


def mm(a, b):
    return jnp.dot(a, b, preferred_element_type=F32)


def left_apply(table_ref, value):
    rows = table_ref.shape[0] // 2
    high, low = split(value)
    both = mm(table_ref[...], high)
    return both[:rows] + both[rows:] + mm(table_ref[:rows, :], low)


def swap_parts(value, sign):
    half = value.shape[1] // 2
    lane = lax.broadcasted_iota(jnp.int32, value.shape, 1)
    rolled = pltpu.roll(value, half, 1)
    return jnp.where(lane < half, sign * rolled, -sign * rolled)


def to_waves(table_ref, value):
    both = left_apply(table_ref, value)
    return both[:KB] + swap_parts(both[KB:], 1.0)


def to_points(table_ref, value):
    return left_apply(table_ref, jnp.concatenate([value, swap_parts(value, -1.0)], axis=0))


def spread(orb, owners, src, half, work, near, far, ssem, rsem):
    points = orb.shape[1]
    part = points // 2
    band = lax.axis_index("band")
    bits = [lax.rem(band, 2), lax.rem(band // 2, 2), band // 4]
    other = [band + weight * (1 - 2 * bit) for weight, bit in zip((1, 2, 4), bits)]
    mine = bits[0] * part
    axes = ((1, 2), (2, 1))

    def rows(start, size):
        return pl.ds(pl.multiple_of(start, 8), size)

    def local(which):
        one, two = axes[which]
        keep = which * (part // 2) + bits[one] * (part // 4)
        drop = which * (part // 2) + (1 - bits[one]) * (part // 4)
        last = keep + bits[two] * (part // 8)
        give = keep + (1 - bits[two]) * (part // 8)
        return keep, drop, last, give

    def copy(source, target, chunk, number, axis):
        return pltpu.make_async_remote_copy(
            source, target, ssem.at[chunk, number], rsem.at[chunk, number],
            device_id={"band": other[axis]}, device_id_type=pl.DeviceIdType.MESH,
        )

    def choose(source, axis, kept, arrived):
        owner = jnp.zeros(kept.shape, jnp.int32) + owners[source]
        return jnp.where(((owner >> axis) & 1) == bits[axis], kept, arrived)

    def start(chunk, stage):
        span = pl.ds(chunk * ROWS, ROWS)
        if stage == 0:
            source = orb.at[span, rows((1 - bits[0]) * part, part)]
            copies = [copy(source, half.at[span], chunk, 0, 0)]
        else:
            copies = []
            for which in range(2):
                one, two = axes[which]
                keep, drop, last, give = local(which)
                number = 1 + which * 5 + stage - 1
                if stage == 1:
                    source = work.at[:, span, rows(drop, part // 4)]
                    made = copy(source, near.at[which, :, span], chunk, number, one)
                elif stage == 2:
                    source = work.at[:, span, rows(give, part // 8)]
                    made = copy(source, far.at[which, :, span], chunk, number, two)
                else:
                    if stage == 3:
                        begin, size, axis = last, part // 8, two
                    elif stage == 4:
                        begin, size, axis = keep, part // 4, one
                    else:
                        begin, size, axis = which * (part // 2), part // 2, 0
                    place = src.at[:, span, rows(mine + begin, size)]
                    made = copy(place, place, chunk, number, axis)
                copies.append(made)
        for made in copies:
            made.start()
        return copies

    def resolve(chunk, stage):
        span = pl.ds(chunk * ROWS, ROWS)
        for source in range(2):
            if stage == 0:
                kept = orb[span, rows(mine, part), :]
                work[source, span] = choose(source, 0, kept, half[span])
                continue
            for which in range(2):
                one, two = axes[which]
                keep, drop, last, give = local(which)
                if stage == 1:
                    place = rows(keep, part // 4)
                    kept = work[source, span, place, :]
                    work[source, span, place, :] = choose(source, one, kept, near[which, source, span])
                elif stage == 2:
                    kept = work[source, span, rows(last, part // 8), :]
                    arrived = far[which, source, span]
                    src[source, span, rows(mine + last, part // 8), :] = choose(source, two, kept, arrived)

    return other, start, resolve


def kernel(slabs, spreading, *refs):
    if spreading:
        orb, owners, ids, fw, bw, zih, zil, zoh, zol, exch, energy = refs[:11]
        send1, recv1, send2, recv2, powers, s1, r1, s2, r2, sp, rp, own = refs[11:23]
        src, half, work, near, far, ssem, rsem = refs[23:]
        others, start, resolve = spread(orb, owners, src, half, work, near, far, ssem, rsem)
    else:
        orb, src, ids, fw, bw, zih, zil, zoh, zol, exch, energy = refs[:11]
        send1, recv1, send2, recv2, powers, s1, r1, s2, r2, sp, rp, own = refs[11:]
        others = []
    planes, points = orb.shape[0], orb.shape[1]
    chunks = planes // ROWS
    width = KB // slabs
    me = lax.axis_index("slab")

    def peer(step):
        return {"slab": lax.rem(me + step, slabs)}

    barrier = pltpu.get_barrier_semaphore()
    for step in range(1, slabs):
        pl.semaphore_signal(barrier, inc=1, device_id=peer(step), device_id_type=pl.DeviceIdType.MESH)
    for device in others:
        pl.semaphore_signal(
            barrier, inc=1, device_id={"band": device}, device_id_type=pl.DeviceIdType.MESH
        )
    pl.semaphore_wait(barrier, slabs - 1 + len(others))

    forward = []

    def advance(chunk):

        def group(part, carry, chunk=chunk):
            base = chunk * ROWS + part * 4
            here = orb[pl.ds(base, 4)].reshape(4 * points, points)
            h0, l0 = split(src[0, pl.ds(base, 4)].reshape(4 * points, points) * here)
            h1, l1 = split(src[1, pl.ds(base, 4)].reshape(4 * points, points) * here)
            high = jnp.concatenate([h0, h1], axis=1)
            low = jnp.concatenate([l0, l1], axis=1)
            along_z = mm(high, zih[...]) + mm(low, zih[...]) + mm(high, zil[...])
            for q in range(4):
                waves = to_waves(fw, along_z[q * points : (q + 1) * points])
                send1[pl.ds(chunk * KB * ROWS + part * 4 + q, KB, stride=ROWS), :] = waves
            return carry

        lax.fori_loop(0, ROWS // 4, group, 0)
        for step in list(range(1, slabs)) + [0]:
            to = lax.rem(me + step, slabs)
            first = pl.multiple_of(chunk * KB * ROWS + to * (width * ROWS), 8)
            source = send1.at[pl.ds(first, width * ROWS)]
            target = recv1.at[me * chunks + chunk]
            if step == 0:
                copy = pltpu.make_async_copy(source, target, own.at[0, chunk])
            else:
                copy = pltpu.make_async_remote_copy(
                    source, target, s1.at[chunk, step], r1.at[chunk, step],
                    device_id=peer(step), device_id_type=pl.DeviceIdType.MESH,
                )
            copy.start()
            forward.append(copy)

    if spreading:
        sent = []
        flying = {}
        for tick in range(chunks + STAGES):
            for stage in reversed(range(STAGES)):
                chunk = tick - stage
                if not 0 <= chunk < chunks:
                    continue
                if stage > 0:
                    for copy in flying[chunk]:
                        copy.wait_recv()
                    resolve(chunk, stage - 1)
                flying[chunk] = start(chunk, stage)
                sent.extend(flying[chunk])
            chunk = tick - STAGES
            if 0 <= chunk < chunks:
                for copy in flying[chunk]:
                    copy.wait_recv()
                advance(chunk)
    else:
        sent = []
        for chunk in range(chunks):
            advance(chunk)
    for copy in forward:
        copy.wait()

    lane_z = lax.broadcasted_iota(jnp.int32, (KB, 2 * KB), 1) & (KH - 1)
    wave_x = lax.broadcasted_iota(jnp.int32, (KB, 2 * KB), 0) - KCUT
    flat = wave_x * wave_x + lane_z * lane_z

    def column(k, carry):
        rows = pl.ds(pl.multiple_of(k * ROWS, ROWS), ROWS)
        spectrum = to_waves(fw, recv1[:, rows, :].reshape(points, 2 * KB))
        wave_y = me * width + k - KCUT
        radius = flat + wave_y * wave_y
        weight = jnp.where(radius < KCUT * KCUT, 4.0 / (1.0 + radius.astype(F32) / 1024.0), 0.0)
        filtered = weight * spectrum
        powers[me, pl.ds(k, 1), :] = jnp.sum(filtered * spectrum, axis=0, keepdims=True)
        send2[:, rows, :] = to_points(bw, filtered).reshape(slabs * chunks, ROWS, 2 * KB)
        return carry

    lax.fori_loop(0, width, column, 0, unroll=4)

    back = []
    for chunk in range(chunks):
        waits = []
        for step in list(range(1, slabs)) + [0]:
            to = lax.rem(me + step, slabs)
            first = pl.multiple_of(chunk * KB * ROWS + me * (width * ROWS), 8)
            source = send2.at[to * chunks + chunk]
            target = recv2.at[pl.ds(first, width * ROWS)]
            if step == 0:
                copy = pltpu.make_async_copy(source, target, own.at[1, chunk])
            else:
                copy = pltpu.make_async_remote_copy(
                    source, target, s2.at[chunk, step], r2.at[chunk, step],
                    device_id=peer(step), device_id_type=pl.DeviceIdType.MESH,
                )
            copy.start()
            waits.append(copy)
        back.append(waits)
        if chunk == 0:
            shared = []
            for step in range(1, slabs):
                copy = pltpu.make_async_remote_copy(
                    powers.at[me], powers.at[me], sp.at[step], rp.at[step],
                    device_id=peer(step), device_id_type=pl.DeviceIdType.MESH,
                )
                copy.start()
                shared.append(copy)
    for copy in shared:
        copy.wait()

    power = powers[...].reshape(KB, 2 * KB) * (1.0 / KB)
    slots = ids[...]
    wave_y = (slots >> 6) - KCUT
    wave_z = (slots & (KB - 1)) - KCUT
    wave_y = jnp.where(wave_z < 0, -wave_y, wave_y)
    wave_z = jnp.where(wave_z < 0, -wave_z, wave_z)
    count = slots.shape[1]
    row = lax.broadcasted_iota(jnp.int32, (KB, count), 0) - KCUT
    pick_y = jnp.where(row == wave_y, 1.0, 0.0).astype(BF16)
    row = lax.broadcasted_iota(jnp.int32, (2 * KB, count), 0) & (KH - 1)
    high, low = split(power.T)
    rows_of = mm(high, pick_y) + mm(low, pick_y)
    energy[...] = jnp.sum(jnp.where(row == wave_z, rows_of, 0.0), axis=0, keepdims=True)

    for chunk in range(chunks):
        for copy in back[chunk]:
            copy.wait()

        def ungroup(part, carry, chunk=chunk):
            base = chunk * ROWS + part * 4
            pieces = []
            for q in range(4):
                waves = recv2[pl.ds(chunk * KB * ROWS + part * 4 + q, KB, stride=ROWS), :]
                pieces.append(to_points(bw, waves))
            high, low = split(jnp.concatenate(pieces, axis=0))
            both = mm(high, zoh[...]) + mm(low, zoh[...]) + mm(high, zol[...])
            first = src[0, pl.ds(base, 4)].reshape(4 * points, points)
            second = src[1, pl.ds(base, 4)].reshape(4 * points, points)
            total = first * both[:, :points] + second * both[:, points:]
            exch[pl.ds(base, 4)] = total.reshape(4, points, points)
            return carry

        lax.fori_loop(0, ROWS // 4, ungroup, 0)
    for copy in sent:
        copy.wait_send()


def from_root(shard, axis, root):
    mine = lax.axis_index(axis) == root
    return lax.psum(jnp.where(mine, shard, jnp.zeros_like(shard)), axis)


def body(orbitals, column_ids, source_ids):
    slabs = lax.axis_size("slab")
    planes, points = orbitals.shape[1], orbitals.shape[2]
    chunks = planes // ROWS
    width = KB // slabs
    bands = lax.axis_size("band")
    spreading = bands == 8 and points % 128 == 0
    vmem = pl.BlockSpec(memory_space=pltpu.VMEM)
    dma = pltpu.SemaphoreType.DMA
    if spreading:
        sources = source_ids
        extra = [
            pltpu.VMEM((2, planes, points, points), F32),
            pltpu.VMEM((planes, points // 2, points), F32),
            pltpu.VMEM((2, planes, points // 2, points), F32),
            pltpu.VMEM((2, 2, planes, points // 8, points), F32),
            pltpu.VMEM((2, 2, planes, points // 16, points), F32),
            dma((chunks, 11)),
            dma((chunks, 11)),
        ]
        place = pl.BlockSpec(memory_space=pltpu.SMEM)
    else:
        sources = jnp.stack([from_root(orbitals[0], "band", source_ids[i]) for i in range(2)])
        extra = []
        place = vmem
    exchange, energy = pl.pallas_call(
        functools.partial(kernel, slabs, spreading),
        out_shape=(
            jax.ShapeDtypeStruct((planes, points, points), F32),
            jax.ShapeDtypeStruct((1, column_ids.shape[1]), F32),
        ),
        in_specs=[vmem, place] + [vmem] * 7,
        out_specs=(vmem, vmem),
        scratch_shapes=[
            pltpu.VMEM((chunks * KB * ROWS, 2 * KB), F32),
            pltpu.VMEM((slabs * chunks, width * ROWS, 2 * KB), F32),
            pltpu.VMEM((slabs * chunks, width * ROWS, 2 * KB), F32),
            pltpu.VMEM((chunks * KB * ROWS, 2 * KB), F32),
            pltpu.VMEM((slabs, width, 2 * KB), F32),
            dma((chunks, slabs)),
            dma((chunks, slabs)),
            dma((chunks, slabs)),
            dma((chunks, slabs)),
            dma((slabs,)),
            dma((slabs,)),
            dma((2, chunks)),
            *extra,
        ],
        compiler_params=pltpu.CompilerParams(
            collective_id=0, has_side_effects=True, vmem_limit_bytes=48 * 1024 * 1024
        ),
        name="exchange_action",
    )(orbitals[0], sources, column_ids, *[jnp.asarray(t) for t in tables(points)])
    return exchange[None], energy


def solution(mesh):
    placed = (P("band", "slab", None, None), P("slab", None), P())
    return jax.shard_map(
        body,
        mesh=mesh,
        in_specs=placed,
        out_specs=(P("band", "slab", None, None), P("band", "slab")),
        check_vma=False,
    )
```

```python
import functools

import jax
import jax.numpy as jnp
import ml_dtypes
import numpy as np
from jax import lax
from jax.experimental import pallas as pl
from jax.experimental.pallas import tpu as pltpu
from jax.sharding import PartitionSpec as P

KCUT = 32
KB = 64
KH = 32
ROWS = 8
STAGES = 6
PIECE = 4
F32 = jnp.float32
BF16 = jnp.bfloat16


def halves(table):
    table = table.astype(np.float32)
    high = table.astype(ml_dtypes.bfloat16)
    low = (table - high.astype(np.float32)).astype(ml_dtypes.bfloat16)
    return high, low


def tables(points):
    wave = np.arange(KB) - KCUT
    angle = (wave[:, None] * np.arange(points)[None, :] % points) * (2.0 * np.pi / points)
    forward = np.concatenate([np.cos(angle), np.sin(angle)], axis=0)
    backward = np.concatenate([np.cos(angle).T, np.sin(angle).T], axis=1)
    angle = (np.arange(KH)[:, None] * np.arange(points)[None, :] % points) * (2.0 * np.pi / points)
    unitary = float(points) ** (-1.5)
    cos_z, sin_z = np.cos(angle) * unitary, np.sin(angle) * unitary
    none = np.zeros_like(cos_z)
    into = np.concatenate(
        [
            np.concatenate([cos_z, none, -sin_z, none], axis=0).T,
            np.concatenate([none, cos_z, none, -sin_z], axis=0).T,
        ],
        axis=0,
    )
    twice = np.where(np.arange(KH) == 0, 1.0, 2.0)[:, None]
    cos_b, sin_b = cos_z * twice, sin_z * twice
    out = np.concatenate(
        [
            np.concatenate([cos_b, none, -sin_b, none], axis=0),
            np.concatenate([none, cos_b, none, -sin_b], axis=0),
        ],
        axis=1,
    )
    fh, fl = halves(forward)
    bh, bl = halves(backward)
    ih, il = halves(into)
    oh, ol = halves(out)
    oh, ol = [np.concatenate(np.split(table, 2, axis=1), axis=0) for table in (oh, ol)]
    return (np.concatenate([fh, fl], 0), np.concatenate([bh, bl], 0), ih, il, oh, ol)


def split(value):
    high = value.astype(BF16)
    return high, (value - high.astype(F32)).astype(BF16)


def mm(a, b):
    return jnp.dot(a, b, preferred_element_type=F32)


def left_apply(table_ref, value):
    rows = table_ref.shape[0] // 2
    high, low = split(value)
    both = mm(table_ref[...], high)
    return both[:rows] + both[rows:] + mm(table_ref[:rows, :], low)


def swap_parts(value, sign):
    half = value.shape[1] // 2
    lane = lax.broadcasted_iota(jnp.int32, value.shape, 1)
    rolled = pltpu.roll(value, half, 1)
    return jnp.where(lane < half, sign * rolled, -sign * rolled)


def to_waves(table_ref, value):
    both = left_apply(table_ref, value)
    return both[:KB] + swap_parts(both[KB:], 1.0)


def to_points(table_ref, value):
    return left_apply(table_ref, jnp.concatenate([value, swap_parts(value, -1.0)], axis=0))


def spread(far_orb, orb, owners, src, half, work, near, far, ssem, rsem):
    points = orb.shape[1]
    part = points // 2
    band = lax.axis_index("band")
    bits = [lax.rem(band, 2), lax.rem(band // 2, 2), band // 4]
    other = [band + weight * (1 - 2 * bit) for weight, bit in zip((1, 2, 4), bits)]
    mine = bits[0] * part
    axes = ((1, 2), (2, 1))

    def rows(start, size):
        return pl.ds(pl.multiple_of(start, 8), size)

    def local(which):
        one, two = axes[which]
        keep = which * (part // 2) + bits[one] * (part // 4)
        drop = which * (part // 2) + (1 - bits[one]) * (part // 4)
        last = keep + bits[two] * (part // 8)
        give = keep + (1 - bits[two]) * (part // 8)
        return keep, drop, last, give

    def copy(source, target, chunk, number, axis):
        return pltpu.make_async_remote_copy(
            source, target, ssem.at[chunk, number], rsem.at[chunk, number],
            device_id={"band": other[axis]}, device_id_type=pl.DeviceIdType.MESH,
        )

    def choose(source, axis, kept, arrived):
        owner = jnp.zeros(kept.shape, jnp.int32) + owners[source]
        return jnp.where(((owner >> axis) & 1) == bits[axis], kept, arrived)

    def start(chunk, stage):
        span = pl.ds(chunk * PIECE, PIECE)
        if stage == 0:
            source = far_orb.at[span, rows((1 - bits[0]) * part, part)]
            copies = [copy(source, half.at[span], chunk, 0, 0)]
        else:
            copies = []
            for which in range(2):
                one, two = axes[which]
                keep, drop, last, give = local(which)
                number = 1 + which * 5 + stage - 1
                if stage == 1:
                    source = work.at[:, span, rows(drop, part // 4)]
                    made = copy(source, near.at[which, :, span], chunk, number, one)
                elif stage == 2:
                    source = work.at[:, span, rows(give, part // 8)]
                    made = copy(source, far.at[which, :, span], chunk, number, two)
                else:
                    if stage == 3:
                        begin, size, axis = last, part // 8, two
                    elif stage == 4:
                        begin, size, axis = keep, part // 4, one
                    else:
                        begin, size, axis = which * (part // 2), part // 2, 0
                    place = src.at[:, span, rows(mine + begin, size)]
                    made = copy(place, place, chunk, number, axis)
                copies.append(made)
        for made in copies:
            made.start()
        return copies

    def resolve(chunk, stage):
        span = pl.ds(chunk * PIECE, PIECE)
        for source in range(2):
            if stage == 0:
                kept = orb[span, rows(mine, part), :]
                work[source, span] = choose(source, 0, kept, half[span])
                continue
            for which in range(2):
                one, two = axes[which]
                keep, drop, last, give = local(which)
                if stage == 1:
                    place = rows(keep, part // 4)
                    kept = work[source, span, place, :]
                    work[source, span, place, :] = choose(source, one, kept, near[which, source, span])
                elif stage == 2:
                    kept = work[source, span, rows(last, part // 8), :]
                    arrived = far[which, source, span]
                    src[source, span, rows(mine + last, part // 8), :] = choose(source, two, kept, arrived)

    return other, start, resolve


def kernel(slabs, spreading, *refs):
    if spreading:
        owners, exch, energy = refs[1], refs[9], refs[10]
        send1, recv1, send2, recv2, powers, s1, r1, s2, r2, sp, rp, own, made, stored = refs[11:25]
        src, half, work, near, far, ssem, rsem = refs[25:32]
        placed, loaded = refs[32:40], refs[40]
        orb, ids, fw, bw, zih, zil, zoh, zol = placed
        outside = (refs[0],) + refs[2:9]
        loads = [
            pltpu.make_async_copy(there, here, loaded.at[number])
            for number, (there, here) in enumerate(zip(outside, placed))
        ]
        for load in loads:
            load.start()
        others, start, resolve = spread(
            refs[0], orb, owners, src, half, work, near, far, ssem, rsem
        )
    else:
        orb, src, ids, fw, bw, zih, zil, zoh, zol, exch, energy = refs[:11]
        send1, recv1, send2, recv2, powers, s1, r1, s2, r2, sp, rp, own, made, stored = refs[11:]
        others = []
    planes, points = orb.shape[0], orb.shape[1]
    chunks = planes // ROWS
    width = KB // slabs
    me = lax.axis_index("slab")

    def peer(step):
        return {"slab": lax.rem(me + step, slabs)}

    barrier = pltpu.get_barrier_semaphore()
    for step in range(1, slabs):
        pl.semaphore_signal(barrier, inc=1, device_id=peer(step), device_id_type=pl.DeviceIdType.MESH)
    for device in others:
        pl.semaphore_signal(
            barrier, inc=1, device_id={"band": device}, device_id_type=pl.DeviceIdType.MESH
        )
    pl.semaphore_wait(barrier, slabs - 1 + len(others))

    forward = []

    def advance(chunk):

        def group(part, carry, chunk=chunk):
            base = chunk * ROWS + part * 4
            here = orb[pl.ds(base, 4)].reshape(4 * points, points)
            h0, l0 = split(src[0, pl.ds(base, 4)].reshape(4 * points, points) * here)
            h1, l1 = split(src[1, pl.ds(base, 4)].reshape(4 * points, points) * here)
            high = jnp.concatenate([h0, h1], axis=1)
            low = jnp.concatenate([l0, l1], axis=1)
            along_z = mm(high, zih[...]) + mm(low, zih[...]) + mm(high, zil[...])
            for q in range(4):
                waves = to_waves(fw, along_z[q * points : (q + 1) * points])
                send1[pl.ds(chunk * KB * ROWS + part * 4 + q, KB, stride=ROWS), :] = waves
            return carry

        lax.fori_loop(0, ROWS // 4, group, 0)
        for step in list(range(1, slabs)) + [0]:
            to = lax.rem(me + step, slabs)
            first = pl.multiple_of(chunk * KB * ROWS + to * (width * ROWS), 8)
            source = send1.at[pl.ds(first, width * ROWS)]
            target = recv1.at[me * chunks + chunk]
            if step == 0:
                copy = pltpu.make_async_copy(source, target, own.at[0, chunk])
            else:
                copy = pltpu.make_async_remote_copy(
                    source, target, s1.at[chunk, step], r1.at[chunk, step],
                    device_id=peer(step), device_id_type=pl.DeviceIdType.MESH,
                )
            copy.start()
            forward.append(copy)

    if spreading:
        sent = []
        flying = {}
        pieces = planes // PIECE
        each = ROWS // PIECE
        for tick in range(pieces + STAGES):
            if tick == 1:
                for load in loads:
                    load.wait()
            for stage in reversed(range(STAGES)):
                chunk = tick - stage
                if not 0 <= chunk < pieces:
                    continue
                if stage > 0:
                    for copy in flying[chunk]:
                        copy.wait_recv()
                    resolve(chunk, stage - 1)
                flying[chunk] = start(chunk, stage)
                sent.extend(flying[chunk])
            chunk = tick - STAGES
            if 0 <= chunk < pieces:
                for copy in flying[chunk]:
                    copy.wait_recv()
                if chunk % each == each - 1:
                    advance(chunk // each)
    else:
        sent = []
        for chunk in range(chunks):
            advance(chunk)
    for copy in forward:
        copy.wait()

    lane_z = lax.broadcasted_iota(jnp.int32, (KB, 2 * KB), 1) & (KH - 1)
    wave_x = lax.broadcasted_iota(jnp.int32, (KB, 2 * KB), 0) - KCUT
    flat = wave_x * wave_x + lane_z * lane_z

    def column(k, carry):
        rows = pl.ds(pl.multiple_of(k * ROWS, ROWS), ROWS)
        spectrum = to_waves(fw, recv1[:, rows, :].reshape(points, 2 * KB))
        wave_y = me * width + k - KCUT
        radius = flat + wave_y * wave_y
        weight = jnp.where(radius < KCUT * KCUT, 4.0 / (1.0 + radius.astype(F32) / 1024.0), 0.0)
        filtered = weight * spectrum
        powers[me, pl.ds(k, 1), :] = jnp.sum(filtered * spectrum, axis=0, keepdims=True)
        send2[:, rows, :] = to_points(bw, filtered).reshape(slabs * chunks, ROWS, 2 * KB)
        return carry

    lax.fori_loop(0, width, column, 0, unroll=4)

    back = []
    for chunk in range(chunks):
        waits = []
        for step in list(range(1, slabs)) + [0]:
            to = lax.rem(me + step, slabs)
            first = pl.multiple_of(chunk * KB * ROWS + me * (width * ROWS), 8)
            source = send2.at[to * chunks + chunk]
            target = recv2.at[pl.ds(first, width * ROWS)]
            if step == 0:
                copy = pltpu.make_async_copy(source, target, own.at[1, chunk])
            else:
                copy = pltpu.make_async_remote_copy(
                    source, target, s2.at[chunk, step], r2.at[chunk, step],
                    device_id=peer(step), device_id_type=pl.DeviceIdType.MESH,
                )
            copy.start()
            waits.append(copy)
        back.append(waits)
        if chunk == 0:
            shared = []
            for step in range(1, slabs):
                copy = pltpu.make_async_remote_copy(
                    powers.at[me], powers.at[me], sp.at[step], rp.at[step],
                    device_id=peer(step), device_id_type=pl.DeviceIdType.MESH,
                )
                copy.start()
                shared.append(copy)
    for copy in shared:
        copy.wait()

    power = powers[...].reshape(KB, 2 * KB) * (1.0 / KB)
    slots = ids[...]
    wave_y = (slots >> 6) - KCUT
    wave_z = (slots & (KB - 1)) - KCUT
    wave_y = jnp.where(wave_z < 0, -wave_y, wave_y)
    wave_z = jnp.where(wave_z < 0, -wave_z, wave_z)
    count = slots.shape[1]
    row = lax.broadcasted_iota(jnp.int32, (KB, count), 0) - KCUT
    pick_y = jnp.where(row == wave_y, 1.0, 0.0).astype(BF16)
    row = lax.broadcasted_iota(jnp.int32, (2 * KB, count), 0) & (KH - 1)
    high, low = split(power.T)
    rows_of = mm(high, pick_y) + mm(low, pick_y)
    energy[...] = jnp.sum(jnp.where(row == wave_z, rows_of, 0.0), axis=0, keepdims=True)

    stores = []
    for chunk in range(chunks):
        for copy in back[chunk]:
            copy.wait()

        def ungroup(part, carry, chunk=chunk):
            base = chunk * ROWS + part * 4
            pieces = []
            for q in range(4):
                waves = recv2[pl.ds(chunk * KB * ROWS + part * 4 + q, KB, stride=ROWS), :]
                pieces.append(to_points(bw, waves))
            high, low = split(jnp.concatenate(pieces, axis=0))
            top = jnp.concatenate([zoh[:points, :], zoh[points:, :]], axis=1)
            rest = jnp.concatenate([zol[:points, :], zol[points:, :]], axis=1)
            both = mm(high, top) + mm(low, top) + mm(high, rest)
            first = src[0, pl.ds(base, 4)].reshape(4 * points, points)
            second = src[1, pl.ds(base, 4)].reshape(4 * points, points)
            total = first * both[:, :points] + second * both[:, points:]
            made[pl.ds(base, 4)] = total.reshape(4, points, points)
            return carry

        lax.fori_loop(0, ROWS // 4, ungroup, 0)
        span = pl.ds(chunk * ROWS, ROWS)
        stores.append(pltpu.make_async_copy(made.at[span], exch.at[span], stored.at[chunk]))
        stores[-1].start()
    for copy in stores:
        copy.wait()
    for copy in sent:
        copy.wait_send()


def from_root(shard, axis, root):
    mine = lax.axis_index(axis) == root
    return lax.psum(jnp.where(mine, shard, jnp.zeros_like(shard)), axis)


def body(orbitals, column_ids, source_ids):
    slabs = lax.axis_size("slab")
    planes, points = orbitals.shape[1], orbitals.shape[2]
    chunks = planes // ROWS
    width = KB // slabs
    bands = lax.axis_size("band")
    spreading = bands == 8 and points % 128 == 0
    vmem = pl.BlockSpec(memory_space=pltpu.VMEM)
    dma = pltpu.SemaphoreType.DMA
    fixed = [jnp.asarray(table) for table in tables(points)]
    if spreading:
        sources = source_ids
        extra = [
            pltpu.VMEM((2, planes, points, points), F32),
            pltpu.VMEM((planes, points // 2, points), F32),
            pltpu.VMEM((2, planes, points // 2, points), F32),
            pltpu.VMEM((2, 2, planes, points // 8, points), F32),
            pltpu.VMEM((2, 2, planes, points // 16, points), F32),
            dma((planes // PIECE, 11)),
            dma((planes // PIECE, 11)),
            pltpu.VMEM((planes, points, points), F32),
            pltpu.VMEM(column_ids.shape, jnp.int32),
            *[pltpu.VMEM(table.shape, BF16) for table in fixed],
            dma((8,)),
        ]
        home = pl.BlockSpec(memory_space=pltpu.HBM)
        place = pl.BlockSpec(memory_space=pltpu.SMEM)
    else:
        sources = jnp.stack([from_root(orbitals[0], "band", source_ids[i]) for i in range(2)])
        extra = []
        home = place = vmem
    exchange, energy = pl.pallas_call(
        functools.partial(kernel, slabs, spreading),
        out_shape=(
            jax.ShapeDtypeStruct((planes, points, points), F32),
            jax.ShapeDtypeStruct((1, column_ids.shape[1]), F32),
        ),
        in_specs=[home, place] + [home] * 7,
        out_specs=(pl.BlockSpec(memory_space=pltpu.HBM), vmem),
        scratch_shapes=[
            pltpu.VMEM((chunks * KB * ROWS, 2 * KB), F32),
            pltpu.VMEM((slabs * chunks, width * ROWS, 2 * KB), F32),
            pltpu.VMEM((slabs * chunks, width * ROWS, 2 * KB), F32),
            pltpu.VMEM((chunks * KB * ROWS, 2 * KB), F32),
            pltpu.VMEM((slabs, width, 2 * KB), F32),
            dma((chunks, slabs)),
            dma((chunks, slabs)),
            dma((chunks, slabs)),
            dma((chunks, slabs)),
            dma((slabs,)),
            dma((slabs,)),
            dma((2, chunks)),
            pltpu.VMEM((planes, points, points), F32),
            dma((chunks,)),
            *extra,
        ],
        compiler_params=pltpu.CompilerParams(
            collective_id=0, has_side_effects=True, vmem_limit_bytes=63 * 1024 * 1024
        ),
        name="exchange_action",
    )(orbitals[0], sources, column_ids, *fixed)
    return exchange[None], energy


def solution(mesh):
    placed = (P("band", "slab", None, None), P("slab", None), P())
    return jax.shard_map(
        body,
        mesh=mesh,
        in_specs=placed,
        out_specs=(P("band", "slab", None, None), P("band", "slab")),
        check_vma=False,
    )
```

```python
import functools

import jax
import jax.numpy as jnp
import ml_dtypes
import numpy as np
from jax import lax
from jax.experimental import pallas as pl
from jax.experimental.pallas import tpu as pltpu
from jax.sharding import PartitionSpec as P

KCUT = 32
KB = 64
KH = 32
ROWS = 8
STAGES = 6
PIECE = 4
F32 = jnp.float32
BF16 = jnp.bfloat16


def halves(table):
    table = table.astype(np.float32)
    high = table.astype(ml_dtypes.bfloat16)
    low = (table - high.astype(np.float32)).astype(ml_dtypes.bfloat16)
    return high, low


def tables(points):
    wave = np.arange(KB) - KCUT
    angle = (wave[:, None] * np.arange(points)[None, :] % points) * (2.0 * np.pi / points)
    forward = np.concatenate([np.cos(angle), np.sin(angle)], axis=0)
    backward = np.concatenate([np.cos(angle).T, np.sin(angle).T], axis=1)
    angle = (np.arange(KH)[:, None] * np.arange(points)[None, :] % points) * (2.0 * np.pi / points)
    unitary = float(points) ** (-1.5)
    cos_z, sin_z = np.cos(angle) * unitary, np.sin(angle) * unitary
    none = np.zeros_like(cos_z)
    into = np.concatenate(
        [
            np.concatenate([cos_z, none, -sin_z, none], axis=0).T,
            np.concatenate([none, cos_z, none, -sin_z], axis=0).T,
        ],
        axis=0,
    )
    twice = np.where(np.arange(KH) == 0, 1.0, 2.0)[:, None]
    cos_b, sin_b = cos_z * twice, sin_z * twice
    out = np.concatenate(
        [
            np.concatenate([cos_b, none, -sin_b, none], axis=0),
            np.concatenate([none, cos_b, none, -sin_b], axis=0),
        ],
        axis=1,
    )
    fh, fl = halves(forward)
    bh, bl = halves(backward)
    ih, il = halves(into)
    oh, ol = halves(out)
    oh, ol = [np.concatenate(np.split(table, 2, axis=1), axis=0) for table in (oh, ol)]
    return (np.concatenate([fh, fl], 0), np.concatenate([bh, bl], 0), ih, il, oh, ol)


def split(value):
    high = value.astype(BF16)
    return high, (value - high.astype(F32)).astype(BF16)


def mm(a, b):
    return jnp.dot(a, b, preferred_element_type=F32)


def left_apply(table_ref, value):
    rows = table_ref.shape[0] // 2
    high, low = split(value)
    both = mm(table_ref[...], high)
    return both[:rows] + both[rows:] + mm(table_ref[:rows, :], low)


def swap_parts(value, sign):
    half = value.shape[1] // 2
    lane = lax.broadcasted_iota(jnp.int32, value.shape, 1)
    rolled = pltpu.roll(value, half, 1)
    return jnp.where(lane < half, sign * rolled, -sign * rolled)


def to_waves(table_ref, value):
    both = left_apply(table_ref, value)
    return both[:KB] + swap_parts(both[KB:], 1.0)


def to_points(table_ref, value):
    return left_apply(table_ref, jnp.concatenate([value, swap_parts(value, -1.0)], axis=0))


def spread(far_orb, orb, owners, src, half, work, near, far, ssem, rsem):
    points = orb.shape[1]
    part = points // 2
    band = lax.axis_index("band")
    bits = [lax.rem(band, 2), lax.rem(band // 2, 2), band // 4]
    other = [band + weight * (1 - 2 * bit) for weight, bit in zip((1, 2, 4), bits)]
    mine = bits[0] * part
    axes = ((1, 2), (2, 1))

    def rows(start, size):
        return pl.ds(pl.multiple_of(start, 8), size)

    def local(which):
        one, two = axes[which]
        keep = which * (part // 2) + bits[one] * (part // 4)
        drop = which * (part // 2) + (1 - bits[one]) * (part // 4)
        last = keep + bits[two] * (part // 8)
        give = keep + (1 - bits[two]) * (part // 8)
        return keep, drop, last, give

    def copy(source, target, chunk, number, axis):
        return pltpu.make_async_remote_copy(
            source, target, ssem.at[chunk, number], rsem.at[chunk, number],
            device_id={"band": other[axis]}, device_id_type=pl.DeviceIdType.MESH,
        )

    def choose(source, axis, kept, arrived):
        owner = jnp.zeros(kept.shape, jnp.int32) + owners[source]
        return jnp.where(((owner >> axis) & 1) == bits[axis], kept, arrived)

    def start(chunk, stage):
        span = pl.ds(chunk * PIECE, PIECE)
        if stage == 0:
            source = far_orb.at[span, rows((1 - bits[0]) * part, part)]
            copies = [copy(source, half.at[span], chunk, 0, 0)]
        else:
            copies = []
            for which in range(2):
                one, two = axes[which]
                keep, drop, last, give = local(which)
                number = 1 + which * 5 + stage - 1
                if stage == 1:
                    source = work.at[:, span, rows(drop, part // 4)]
                    made = copy(source, near.at[which, :, span], chunk, number, one)
                elif stage == 2:
                    source = work.at[:, span, rows(give, part // 8)]
                    made = copy(source, far.at[which, :, span], chunk, number, two)
                else:
                    if stage == 3:
                        begin, size, axis = last, part // 8, two
                    elif stage == 4:
                        begin, size, axis = keep, part // 4, one
                    else:
                        begin, size, axis = which * (part // 2), part // 2, 0
                    place = src.at[:, span, rows(mine + begin, size)]
                    made = copy(place, place, chunk, number, axis)
                copies.append(made)
        for made in copies:
            made.start()
        return copies

    def resolve(chunk, stage):
        span = pl.ds(chunk * PIECE, PIECE)
        for source in range(2):
            if stage == 0:
                kept = orb[span, rows(mine, part), :]
                work[source, span] = choose(source, 0, kept, half[span])
                continue
            for which in range(2):
                one, two = axes[which]
                keep, drop, last, give = local(which)
                if stage == 1:
                    place = rows(keep, part // 4)
                    kept = work[source, span, place, :]
                    work[source, span, place, :] = choose(source, one, kept, near[which, source, span])
                elif stage == 2:
                    kept = work[source, span, rows(last, part // 8), :]
                    arrived = far[which, source, span]
                    src[source, span, rows(mine + last, part // 8), :] = choose(source, two, kept, arrived)

    return other, start, resolve


def kernel(slabs, spreading, *refs):
    if spreading:
        owners, exch, energy = refs[1], refs[9], refs[10]
        send1, recv1, send2, recv2, powers, s1, r1, s2, r2, sp, rp, own, made, stored = refs[11:25]
        src, half, work, near, far, ssem, rsem = refs[25:32]
        placed, loaded = refs[32:40], refs[40]
        orb, ids, fw, bw, zih, zil, zoh, zol = placed
        outside = (refs[0],) + refs[2:9]
        loads = [
            pltpu.make_async_copy(there, here, loaded.at[number])
            for number, (there, here) in enumerate(zip(outside, placed))
        ]
        for load in loads:
            load.start()
        others, start, resolve = spread(
            refs[0], orb, owners, src, half, work, near, far, ssem, rsem
        )
    else:
        orb, src, ids, fw, bw, zih, zil, zoh, zol, exch, energy = refs[:11]
        send1, recv1, send2, recv2, powers, s1, r1, s2, r2, sp, rp, own, made, stored = refs[11:]
        others = []
    planes, points = orb.shape[0], orb.shape[1]
    chunks = planes // ROWS
    width = KB // slabs
    me = lax.axis_index("slab")

    def peer(step):
        return {"slab": lax.rem(me + step, slabs)}

    barrier = pltpu.get_barrier_semaphore()
    for step in range(1, slabs):
        pl.semaphore_signal(barrier, inc=1, device_id=peer(step), device_id_type=pl.DeviceIdType.MESH)
    for device in others:
        pl.semaphore_signal(
            barrier, inc=1, device_id={"band": device}, device_id_type=pl.DeviceIdType.MESH
        )
    pl.semaphore_wait(barrier, slabs - 1 + len(others))

    forward = []

    def advance(chunk):

        def group(part, carry, chunk=chunk):
            base = chunk * ROWS + part * 4
            here = orb[pl.ds(base, 4)].reshape(4 * points, points)
            h0, l0 = split(src[0, pl.ds(base, 4)].reshape(4 * points, points) * here)
            h1, l1 = split(src[1, pl.ds(base, 4)].reshape(4 * points, points) * here)
            high = jnp.concatenate([h0, h1], axis=1)
            low = jnp.concatenate([l0, l1], axis=1)
            along_z = mm(high, zih[...]) + mm(low, zih[...]) + mm(high, zil[...])
            for q in range(4):
                waves = to_waves(fw, along_z[q * points : (q + 1) * points])
                send1[pl.ds(chunk * KB * ROWS + part * 4 + q, KB, stride=ROWS), :] = waves
            return carry

        lax.fori_loop(0, ROWS // 4, group, 0)
        for step in list(range(1, slabs)) + [0]:
            to = lax.rem(me + step, slabs)
            first = pl.multiple_of(chunk * KB * ROWS + to * (width * ROWS), 8)
            source = send1.at[pl.ds(first, width * ROWS)]
            target = recv1.at[me * chunks + chunk]
            if step == 0:
                copy = pltpu.make_async_copy(source, target, own.at[0, chunk])
            else:
                copy = pltpu.make_async_remote_copy(
                    source, target, s1.at[chunk, step], r1.at[chunk, step],
                    device_id=peer(step), device_id_type=pl.DeviceIdType.MESH,
                )
            copy.start()
            forward.append(copy)

    if spreading:
        sent = []
        flying = {}
        pieces = planes // PIECE
        each = ROWS // PIECE
        for tick in range(pieces + STAGES):
            if tick == 1:
                for load in loads:
                    load.wait()
            for stage in reversed(range(STAGES)):
                chunk = tick - stage
                if not 0 <= chunk < pieces:
                    continue
                if stage > 0:
                    for copy in flying[chunk]:
                        copy.wait_recv()
                    resolve(chunk, stage - 1)
                flying[chunk] = start(chunk, stage)
                sent.extend(flying[chunk])
            chunk = tick - STAGES
            if 0 <= chunk < pieces:
                for copy in flying[chunk]:
                    copy.wait_recv()
                if chunk % each == each - 1:
                    advance(chunk // each)
    else:
        sent = []
        for chunk in range(chunks):
            advance(chunk)
    for copy in forward:
        copy.wait()

    lane_z = lax.broadcasted_iota(jnp.int32, (KB, 2 * KB), 1) & (KH - 1)
    wave_x = lax.broadcasted_iota(jnp.int32, (KB, 2 * KB), 0) - KCUT
    flat = wave_x * wave_x + lane_z * lane_z

    def column(k, carry):
        rows = pl.ds(pl.multiple_of(k * ROWS, ROWS), ROWS)
        spectrum = to_waves(fw, recv1[:, rows, :].reshape(points, 2 * KB))
        wave_y = me * width + k - KCUT
        radius = flat + wave_y * wave_y
        weight = jnp.where(radius < KCUT * KCUT, 4.0 / (1.0 + radius.astype(F32) / 1024.0), 0.0)
        filtered = weight * spectrum
        powers[me, pl.ds(k, 1), :] = jnp.sum(filtered * spectrum, axis=0, keepdims=True)
        send2[:, rows, :] = to_points(bw, filtered).reshape(slabs * chunks, ROWS, 2 * KB)
        return carry

    back = [[] for _ in range(chunks)]
    few = width // 2
    for turn in range(2):
        lax.fori_loop(turn * few, (turn + 1) * few, column, 0, unroll=4)
        for chunk in range(chunks):
            for step in list(range(1, slabs)) + [0]:
                to = lax.rem(me + step, slabs)
                begin = chunk * KB * ROWS + me * (width * ROWS) + turn * (few * ROWS)
                source = send2.at[to * chunks + chunk, pl.ds(turn * few * ROWS, few * ROWS)]
                target = recv2.at[pl.ds(pl.multiple_of(begin, 8), few * ROWS)]
                if step == 0:
                    copy = pltpu.make_async_copy(source, target, own.at[1 + turn, chunk])
                else:
                    copy = pltpu.make_async_remote_copy(
                        source, target, s2.at[turn * chunks + chunk, step],
                        r2.at[turn * chunks + chunk, step],
                        device_id=peer(step), device_id_type=pl.DeviceIdType.MESH,
                    )
                copy.start()
                back[chunk].append(copy)
    shared = []
    for step in range(1, slabs):
        copy = pltpu.make_async_remote_copy(
            powers.at[me], powers.at[me], sp.at[step], rp.at[step],
            device_id=peer(step), device_id_type=pl.DeviceIdType.MESH,
        )
        copy.start()
        shared.append(copy)
    for copy in shared:
        copy.wait()

    power = powers[...].reshape(KB, 2 * KB) * (1.0 / KB)
    slots = ids[...]
    wave_y = (slots >> 6) - KCUT
    wave_z = (slots & (KB - 1)) - KCUT
    wave_y = jnp.where(wave_z < 0, -wave_y, wave_y)
    wave_z = jnp.where(wave_z < 0, -wave_z, wave_z)
    count = slots.shape[1]
    row = lax.broadcasted_iota(jnp.int32, (KB, count), 0) - KCUT
    pick_y = jnp.where(row == wave_y, 1.0, 0.0).astype(BF16)
    row = lax.broadcasted_iota(jnp.int32, (2 * KB, count), 0) & (KH - 1)
    high, low = split(power.T)
    rows_of = mm(high, pick_y) + mm(low, pick_y)
    energy[...] = jnp.sum(jnp.where(row == wave_z, rows_of, 0.0), axis=0, keepdims=True)

    stores = []
    for chunk in range(chunks):
        for copy in back[chunk]:
            copy.wait()

        def ungroup(part, carry, chunk=chunk):
            base = chunk * ROWS + part * 4
            pieces = []
            for q in range(4):
                waves = recv2[pl.ds(chunk * KB * ROWS + part * 4 + q, KB, stride=ROWS), :]
                pieces.append(to_points(bw, waves))
            high, low = split(jnp.concatenate(pieces, axis=0))
            top = jnp.concatenate([zoh[:points, :], zoh[points:, :]], axis=1)
            rest = jnp.concatenate([zol[:points, :], zol[points:, :]], axis=1)
            both = mm(high, top) + mm(low, top) + mm(high, rest)
            first = src[0, pl.ds(base, 4)].reshape(4 * points, points)
            second = src[1, pl.ds(base, 4)].reshape(4 * points, points)
            total = first * both[:, :points] + second * both[:, points:]
            made[pl.ds(base, 4)] = total.reshape(4, points, points)
            return carry

        lax.fori_loop(0, ROWS // 4, ungroup, 0)
        span = pl.ds(chunk * ROWS, ROWS)
        stores.append(pltpu.make_async_copy(made.at[span], exch.at[span], stored.at[chunk]))
        stores[-1].start()
    for copy in stores:
        copy.wait()
    for copy in sent:
        copy.wait_send()


def from_root(shard, axis, root):
    mine = lax.axis_index(axis) == root
    return lax.psum(jnp.where(mine, shard, jnp.zeros_like(shard)), axis)


def body(orbitals, column_ids, source_ids):
    slabs = lax.axis_size("slab")
    planes, points = orbitals.shape[1], orbitals.shape[2]
    chunks = planes // ROWS
    width = KB // slabs
    bands = lax.axis_size("band")
    spreading = bands == 8 and points % 128 == 0
    vmem = pl.BlockSpec(memory_space=pltpu.VMEM)
    dma = pltpu.SemaphoreType.DMA
    fixed = [jnp.asarray(table) for table in tables(points)]
    if spreading:
        sources = source_ids
        extra = [
            pltpu.VMEM((2, planes, points, points), F32),
            pltpu.VMEM((planes, points // 2, points), F32),
            pltpu.VMEM((2, planes, points // 2, points), F32),
            pltpu.VMEM((2, 2, planes, points // 8, points), F32),
            pltpu.VMEM((2, 2, planes, points // 16, points), F32),
            dma((planes // PIECE, 11)),
            dma((planes // PIECE, 11)),
            pltpu.VMEM((planes, points, points), F32),
            pltpu.VMEM(column_ids.shape, jnp.int32),
            *[pltpu.VMEM(table.shape, BF16) for table in fixed],
            dma((8,)),
        ]
        home = pl.BlockSpec(memory_space=pltpu.HBM)
        place = pl.BlockSpec(memory_space=pltpu.SMEM)
    else:
        sources = jnp.stack([from_root(orbitals[0], "band", source_ids[i]) for i in range(2)])
        extra = []
        home = place = vmem
    exchange, energy = pl.pallas_call(
        functools.partial(kernel, slabs, spreading),
        out_shape=(
            jax.ShapeDtypeStruct((planes, points, points), F32),
            jax.ShapeDtypeStruct((1, column_ids.shape[1]), F32),
        ),
        in_specs=[home, place] + [home] * 7,
        out_specs=(pl.BlockSpec(memory_space=pltpu.HBM), vmem),
        scratch_shapes=[
            pltpu.VMEM((chunks * KB * ROWS, 2 * KB), F32),
            pltpu.VMEM((slabs * chunks, width * ROWS, 2 * KB), F32),
            pltpu.VMEM((slabs * chunks, width * ROWS, 2 * KB), F32),
            pltpu.VMEM((chunks * KB * ROWS, 2 * KB), F32),
            pltpu.VMEM((slabs, width, 2 * KB), F32),
            dma((chunks, slabs)),
            dma((chunks, slabs)),
            dma((2 * chunks, slabs)),
            dma((2 * chunks, slabs)),
            dma((slabs,)),
            dma((slabs,)),
            dma((3, chunks)),
            pltpu.VMEM((planes, points, points), F32),
            dma((chunks,)),
            *extra,
        ],
        compiler_params=pltpu.CompilerParams(
            collective_id=0, has_side_effects=True, vmem_limit_bytes=63 * 1024 * 1024
        ),
        name="exchange_action",
    )(orbitals[0], sources, column_ids, *fixed)
    return exchange[None], energy


def solution(mesh):
    placed = (P("band", "slab", None, None), P("slab", None), P())
    return jax.shard_map(
        body,
        mesh=mesh,
        in_specs=placed,
        out_specs=(P("band", "slab", None, None), P("band", "slab")),
        check_vma=False,
    )
```

```python
import functools

import jax
import jax.numpy as jnp
import ml_dtypes
import numpy as np
from jax import lax
from jax.experimental import pallas as pl
from jax.experimental.pallas import tpu as pltpu
from jax.sharding import PartitionSpec as P

KCUT = 32
KB = 64
KH = 32
ROWS = 8
STAGES = 6
PIECE = 8
F32 = jnp.float32
BF16 = jnp.bfloat16


def halves(table):
    table = table.astype(np.float32)
    high = table.astype(ml_dtypes.bfloat16)
    low = (table - high.astype(np.float32)).astype(ml_dtypes.bfloat16)
    return high, low


def tables(points):
    wave = np.arange(KB) - KCUT
    angle = (wave[:, None] * np.arange(points)[None, :] % points) * (2.0 * np.pi / points)
    forward = np.concatenate([np.cos(angle), np.sin(angle)], axis=0)
    backward = np.concatenate([np.cos(angle).T, np.sin(angle).T], axis=1)
    angle = (np.arange(KH)[:, None] * np.arange(points)[None, :] % points) * (2.0 * np.pi / points)
    unitary = float(points) ** (-1.5)
    cos_z, sin_z = np.cos(angle) * unitary, np.sin(angle) * unitary
    none = np.zeros_like(cos_z)
    into = np.concatenate(
        [
            np.concatenate([cos_z, none, -sin_z, none], axis=0).T,
            np.concatenate([none, cos_z, none, -sin_z], axis=0).T,
        ],
        axis=0,
    )
    twice = np.where(np.arange(KH) == 0, 1.0, 2.0)[:, None]
    cos_b, sin_b = cos_z * twice, sin_z * twice
    out = np.concatenate(
        [
            np.concatenate([cos_b, none, -sin_b, none], axis=0),
            np.concatenate([none, cos_b, none, -sin_b], axis=0),
        ],
        axis=1,
    )
    fh, fl = halves(forward)
    bh, bl = halves(backward)
    ih, il = halves(into)
    oh, ol = halves(out)
    oh, ol = [np.concatenate(np.split(table, 2, axis=1), axis=0) for table in (oh, ol)]
    return (np.concatenate([fh, fl], 0), np.concatenate([bh, bl], 0), ih, il, oh, ol)


def split(value):
    high = value.astype(BF16)
    return high, (value - high.astype(F32)).astype(BF16)


def mm(a, b):
    return jnp.dot(a, b, preferred_element_type=F32)


def left_apply(table_ref, value):
    rows = table_ref.shape[0] // 2
    high, low = split(value)
    both = mm(table_ref[...], high)
    return both[:rows] + both[rows:] + mm(table_ref[:rows, :], low)


def swap_parts(value, sign):
    half = value.shape[1] // 2
    lane = lax.broadcasted_iota(jnp.int32, value.shape, 1)
    rolled = pltpu.roll(value, half, 1)
    return jnp.where(lane < half, sign * rolled, -sign * rolled)


def to_waves(table_ref, value):
    both = left_apply(table_ref, value)
    return both[:KB] + swap_parts(both[KB:], 1.0)


def to_points(table_ref, value):
    return left_apply(table_ref, jnp.concatenate([value, swap_parts(value, -1.0)], axis=0))


def spread(far_orb, orb, owners, src, half, work, near, far, ssem, rsem):
    points = orb.shape[1]
    part = points // 2
    band = lax.axis_index("band")
    bits = [lax.rem(band, 2), lax.rem(band // 2, 2), band // 4]
    other = [band + weight * (1 - 2 * bit) for weight, bit in zip((1, 2, 4), bits)]
    mine = bits[0] * part
    axes = ((1, 2), (2, 1))

    def rows(start, size):
        return pl.ds(pl.multiple_of(start, 8), size)

    def local(which):
        one, two = axes[which]
        keep = which * (part // 2) + bits[one] * (part // 4)
        drop = which * (part // 2) + (1 - bits[one]) * (part // 4)
        last = keep + bits[two] * (part // 8)
        give = keep + (1 - bits[two]) * (part // 8)
        return keep, drop, last, give

    def copy(source, target, chunk, number, axis):
        return pltpu.make_async_remote_copy(
            source, target, ssem.at[chunk, number], rsem.at[chunk, number],
            device_id={"band": other[axis]}, device_id_type=pl.DeviceIdType.MESH,
        )

    def choose(source, axis, kept, arrived):
        owner = jnp.zeros(kept.shape, jnp.int32) + owners[source]
        return jnp.where(((owner >> axis) & 1) == bits[axis], kept, arrived)

    def start(chunk, stage):
        span = pl.ds(chunk * PIECE, PIECE)
        if stage == 0:
            source = far_orb.at[span, rows((1 - bits[0]) * part, part)]
            copies = [copy(source, half.at[span], chunk, 0, 0)]
        else:
            copies = []
            for which in range(2):
                one, two = axes[which]
                keep, drop, last, give = local(which)
                number = 1 + which * 5 + stage - 1
                if stage == 1:
                    source = work.at[:, span, rows(drop, part // 4)]
                    made = copy(source, near.at[which, :, span], chunk, number, one)
                elif stage == 2:
                    source = work.at[:, span, rows(give, part // 8)]
                    made = copy(source, far.at[which, :, span], chunk, number, two)
                else:
                    if stage == 3:
                        begin, size, axis = last, part // 8, two
                    elif stage == 4:
                        begin, size, axis = keep, part // 4, one
                    else:
                        begin, size, axis = which * (part // 2), part // 2, 0
                    place = src.at[:, span, rows(mine + begin, size)]
                    made = copy(place, place, chunk, number, axis)
                copies.append(made)
        for made in copies:
            made.start()
        return copies

    def resolve(chunk, stage):
        span = pl.ds(chunk * PIECE, PIECE)
        for source in range(2):
            if stage == 0:
                kept = orb[span, rows(mine, part), :]
                work[source, span] = choose(source, 0, kept, half[span])
                continue
            for which in range(2):
                one, two = axes[which]
                keep, drop, last, give = local(which)
                if stage == 1:
                    place = rows(keep, part // 4)
                    kept = work[source, span, place, :]
                    work[source, span, place, :] = choose(source, one, kept, near[which, source, span])
                elif stage == 2:
                    kept = work[source, span, rows(last, part // 8), :]
                    arrived = far[which, source, span]
                    src[source, span, rows(mine + last, part // 8), :] = choose(source, two, kept, arrived)

    return other, start, resolve


def kernel(slabs, spreading, *refs):
    if spreading:
        owners, exch, energy = refs[1], refs[9], refs[10]
        send1, recv1, send2, recv2, powers, s1, r1, s2, r2, sp, rp, own, made, stored = refs[11:25]
        src, half, work, near, far, ssem, rsem = refs[25:32]
        placed, loaded = refs[32:40], refs[40]
        orb, ids, fw, bw, zih, zil, zoh, zol = placed
        outside = (refs[0],) + refs[2:9]
        loads = [
            pltpu.make_async_copy(there, here, loaded.at[number])
            for number, (there, here) in enumerate(zip(outside, placed))
        ]
        for load in loads:
            load.start()
        others, start, resolve = spread(
            refs[0], orb, owners, src, half, work, near, far, ssem, rsem
        )
    else:
        orb, src, ids, fw, bw, zih, zil, zoh, zol, exch, energy = refs[:11]
        send1, recv1, send2, recv2, powers, s1, r1, s2, r2, sp, rp, own, made, stored = refs[11:]
        others = []
    planes, points = orb.shape[0], orb.shape[1]
    chunks = planes // ROWS
    width = KB // slabs
    me = lax.axis_index("slab")

    def peer(step):
        return {"slab": lax.rem(me + step, slabs)}

    barrier = pltpu.get_barrier_semaphore()
    for step in range(1, slabs):
        pl.semaphore_signal(barrier, inc=1, device_id=peer(step), device_id_type=pl.DeviceIdType.MESH)
    for device in others:
        pl.semaphore_signal(
            barrier, inc=1, device_id={"band": device}, device_id_type=pl.DeviceIdType.MESH
        )
    pl.semaphore_wait(barrier, slabs - 1 + len(others))

    forward = []

    def advance(chunk):

        def group(part, carry, chunk=chunk):
            base = chunk * ROWS + part * 4
            here = orb[pl.ds(base, 4)].reshape(4 * points, points)
            h0, l0 = split(src[0, pl.ds(base, 4)].reshape(4 * points, points) * here)
            h1, l1 = split(src[1, pl.ds(base, 4)].reshape(4 * points, points) * here)
            high = jnp.concatenate([h0, h1], axis=1)
            low = jnp.concatenate([l0, l1], axis=1)
            along_z = mm(high, zih[...]) + mm(low, zih[...]) + mm(high, zil[...])
            for q in range(4):
                waves = to_waves(fw, along_z[q * points : (q + 1) * points])
                send1[pl.ds(chunk * KB * ROWS + part * 4 + q, KB, stride=ROWS), :] = waves
            return carry

        lax.fori_loop(0, ROWS // 4, group, 0)
        for step in list(range(1, slabs)) + [0]:
            to = lax.rem(me + step, slabs)
            first = pl.multiple_of(chunk * KB * ROWS + to * (width * ROWS), 8)
            source = send1.at[pl.ds(first, width * ROWS)]
            target = recv1.at[me * chunks + chunk]
            if step == 0:
                copy = pltpu.make_async_copy(source, target, own.at[0, chunk])
            else:
                copy = pltpu.make_async_remote_copy(
                    source, target, s1.at[chunk, step], r1.at[chunk, step],
                    device_id=peer(step), device_id_type=pl.DeviceIdType.MESH,
                )
            copy.start()
            forward.append(copy)

    if spreading:
        sent = []
        flying = {}
        pieces = planes // PIECE
        each = ROWS // PIECE
        for tick in range(pieces + STAGES):
            if tick == 1:
                for load in loads:
                    load.wait()
            for stage in reversed(range(STAGES)):
                chunk = tick - stage
                if not 0 <= chunk < pieces:
                    continue
                if stage > 0:
                    for copy in flying[chunk]:
                        copy.wait_recv()
                    resolve(chunk, stage - 1)
                flying[chunk] = start(chunk, stage)
                sent.extend(flying[chunk])
            chunk = tick - STAGES
            if 0 <= chunk < pieces:
                for copy in flying[chunk]:
                    copy.wait_recv()
                if chunk % each == each - 1:
                    advance(chunk // each)
    else:
        sent = []
        for chunk in range(chunks):
            advance(chunk)
    for copy in forward:
        copy.wait()

    lane_z = lax.broadcasted_iota(jnp.int32, (KB, 2 * KB), 1) & (KH - 1)
    wave_x = lax.broadcasted_iota(jnp.int32, (KB, 2 * KB), 0) - KCUT
    flat = wave_x * wave_x + lane_z * lane_z

    def column(k, carry):
        rows = pl.ds(pl.multiple_of(k * ROWS, ROWS), ROWS)
        spectrum = to_waves(fw, recv1[:, rows, :].reshape(points, 2 * KB))
        wave_y = me * width + k - KCUT
        radius = flat + wave_y * wave_y
        weight = jnp.where(radius < KCUT * KCUT, 4.0 / (1.0 + radius.astype(F32) / 1024.0), 0.0)
        filtered = weight * spectrum
        powers[me, pl.ds(k, 1), :] = jnp.sum(filtered * spectrum, axis=0, keepdims=True)
        send2[:, rows, :] = to_points(bw, filtered).reshape(slabs * chunks, ROWS, 2 * KB)
        return carry

    lax.fori_loop(0, width, column, 0, unroll=4)

    back = []
    for chunk in range(chunks):
        waits = []
        for step in list(range(1, slabs)) + [0]:
            to = lax.rem(me + step, slabs)
            first = pl.multiple_of(chunk * KB * ROWS + me * (width * ROWS), 8)
            source = send2.at[to * chunks + chunk]
            target = recv2.at[pl.ds(first, width * ROWS)]
            if step == 0:
                copy = pltpu.make_async_copy(source, target, own.at[1, chunk])
            else:
                copy = pltpu.make_async_remote_copy(
                    source, target, s2.at[chunk, step], r2.at[chunk, step],
                    device_id=peer(step), device_id_type=pl.DeviceIdType.MESH,
                )
            copy.start()
            waits.append(copy)
        back.append(waits)
        if chunk == 0:
            shared = []
            for step in range(1, slabs):
                copy = pltpu.make_async_remote_copy(
                    powers.at[me], powers.at[me], sp.at[step], rp.at[step],
                    device_id=peer(step), device_id_type=pl.DeviceIdType.MESH,
                )
                copy.start()
                shared.append(copy)
    for copy in shared:
        copy.wait()

    power = powers[...].reshape(KB, 2 * KB) * (1.0 / KB)
    slots = ids[...]
    wave_y = (slots >> 6) - KCUT
    wave_z = (slots & (KB - 1)) - KCUT
    wave_y = jnp.where(wave_z < 0, -wave_y, wave_y)
    wave_z = jnp.where(wave_z < 0, -wave_z, wave_z)
    count = slots.shape[1]
    row = lax.broadcasted_iota(jnp.int32, (KB, count), 0) - KCUT
    pick_y = jnp.where(row == wave_y, 1.0, 0.0).astype(BF16)
    row = lax.broadcasted_iota(jnp.int32, (2 * KB, count), 0) & (KH - 1)
    high, low = split(power.T)
    rows_of = mm(high, pick_y) + mm(low, pick_y)
    energy[...] = jnp.sum(jnp.where(row == wave_z, rows_of, 0.0), axis=0, keepdims=True)

    stores = []
    for chunk in range(chunks):
        for copy in back[chunk]:
            copy.wait()

        def ungroup(part, carry, chunk=chunk):
            base = chunk * ROWS + part * 4
            pieces = []
            for q in range(4):
                waves = recv2[pl.ds(chunk * KB * ROWS + part * 4 + q, KB, stride=ROWS), :]
                pieces.append(to_points(bw, waves))
            high, low = split(jnp.concatenate(pieces, axis=0))
            top = jnp.concatenate([zoh[:points, :], zoh[points:, :]], axis=1)
            rest = jnp.concatenate([zol[:points, :], zol[points:, :]], axis=1)
            both = mm(high, top) + mm(low, top) + mm(high, rest)
            first = src[0, pl.ds(base, 4)].reshape(4 * points, points)
            second = src[1, pl.ds(base, 4)].reshape(4 * points, points)
            total = first * both[:, :points] + second * both[:, points:]
            made[pl.ds(base, 4)] = total.reshape(4, points, points)
            return carry

        lax.fori_loop(0, ROWS // 4, ungroup, 0)
        span = pl.ds(chunk * ROWS, ROWS)
        stores.append(pltpu.make_async_copy(made.at[span], exch.at[span], stored.at[chunk]))
        stores[-1].start()
    for copy in stores:
        copy.wait()
    for copy in sent:
        copy.wait_send()


def from_root(shard, axis, root):
    mine = lax.axis_index(axis) == root
    return lax.psum(jnp.where(mine, shard, jnp.zeros_like(shard)), axis)


def body(orbitals, column_ids, source_ids):
    slabs = lax.axis_size("slab")
    planes, points = orbitals.shape[1], orbitals.shape[2]
    chunks = planes // ROWS
    width = KB // slabs
    bands = lax.axis_size("band")
    spreading = bands == 8 and points % 128 == 0
    vmem = pl.BlockSpec(memory_space=pltpu.VMEM)
    dma = pltpu.SemaphoreType.DMA
    fixed = [jnp.asarray(table) for table in tables(points)]
    if spreading:
        sources = source_ids
        extra = [
            pltpu.VMEM((2, planes, points, points), F32),
            pltpu.VMEM((planes, points // 2, points), F32),
            pltpu.VMEM((2, planes, points // 2, points), F32),
            pltpu.VMEM((2, 2, planes, points // 8, points), F32),
            pltpu.VMEM((2, 2, planes, points // 16, points), F32),
            dma((planes // PIECE, 11)),
            dma((planes // PIECE, 11)),
            pltpu.VMEM((planes, points, points), F32),
            pltpu.VMEM(column_ids.shape, jnp.int32),
            *[pltpu.VMEM(table.shape, BF16) for table in fixed],
            dma((8,)),
        ]
        home = pl.BlockSpec(memory_space=pltpu.HBM)
        place = pl.BlockSpec(memory_space=pltpu.SMEM)
    else:
        sources = jnp.stack([from_root(orbitals[0], "band", source_ids[i]) for i in range(2)])
        extra = []
        home = place = vmem
    exchange, energy = pl.pallas_call(
        functools.partial(kernel, slabs, spreading),
        out_shape=(
            jax.ShapeDtypeStruct((planes, points, points), F32),
            jax.ShapeDtypeStruct((1, column_ids.shape[1]), F32),
        ),
        in_specs=[home, place] + [home] * 7,
        out_specs=(pl.BlockSpec(memory_space=pltpu.HBM), vmem),
        scratch_shapes=[
            pltpu.VMEM((chunks * KB * ROWS, 2 * KB), F32),
            pltpu.VMEM((slabs * chunks, width * ROWS, 2 * KB), F32),
            pltpu.VMEM((slabs * chunks, width * ROWS, 2 * KB), F32),
            pltpu.VMEM((chunks * KB * ROWS, 2 * KB), F32),
            pltpu.VMEM((slabs, width, 2 * KB), F32),
            dma((chunks, slabs)),
            dma((chunks, slabs)),
            dma((chunks, slabs)),
            dma((chunks, slabs)),
            dma((slabs,)),
            dma((slabs,)),
            dma((2, chunks)),
            pltpu.VMEM((planes, points, points), F32),
            dma((chunks,)),
            *extra,
        ],
        compiler_params=pltpu.CompilerParams(
            collective_id=0, has_side_effects=True, vmem_limit_bytes=63 * 1024 * 1024
        ),
        name="exchange_action",
    )(orbitals[0], sources, column_ids, *fixed)
    return exchange[None], energy


def solution(mesh):
    placed = (P("band", "slab", None, None), P("slab", None), P())
    return jax.shard_map(
        body,
        mesh=mesh,
        in_specs=placed,
        out_specs=(P("band", "slab", None, None), P("band", "slab")),
        check_vma=False,
    )
```
